128 devices in a mesh: sub: 2 (over z_hi), row: 8 (over x, z_lo), col: 8 (over y, core).
Axes of the slice: x: 4, y: 4, z: 4 (z_hi: 2, z_lo: 2; z = z_hi * 2 + z_lo), core: 2. Of those that a mesh axis runs over, the one named last changes fastest.
Arguments:
- top_inverse: float32 [4096, 4096], P(('sub', 'row'), 'col'), may hold values from -1 to 4, as said below
- ancestors: int32 [2, 1024], replicated, may hold values from 0 to 4095, as said below
- child_panel: float32 [2, 1024, 3072], P('sub', 'row', 'col'), may hold values from -0.109375 to 0.109375
- child_inverse: float32 [2, 3072, 3072], P('sub', 'row', 'col'), may hold values from -1 to 3, as said below
Outputs:
- top_block: float32 [4096, 4096], P(('sub', 'row'), 'col')
- cross_block: float32 [2, 1024, 3072], P('sub', 'row', 'col')
- child_block: float32 [2, 3072, 3072], P('sub', 'row', 'col')
The draws below stay inside these ranges and needn't reach their ends.
Inputs may be any that keep to these rules, and one draw needn't show every extreme that they name: `ancestors`: each row lists 1024 distinct rows of the top separator in increasing order, always including the first and the last. `top_inverse`: zero above the diagonal, positive diagonal. `child_inverse`: each block zero above the diagonal, positive diagonal.
All inputs are finite; a program needn't handle non-finite values.
Results may differ from the reference program's by a relative error of at most 0.00014.
Values sent between devices are 32-bit elements; how exact they have to be, the bound alone decides.
No kernel may reach another device: no remote copies, remote signals or barrier semaphores. Data moves between devices by JAX's collectives and lax.ppermute only.
A program may use at most 128 MiB of HBM per device.

```python
import math
import jax
import jax.numpy as jnp
from jax import lax

S = 4096
R = 1024
C = 3072
KIDS = 2


def lower_factor(diag_key, rough_part, low_value, high_value):
    matrix_order = rough_part.shape[-1]
    diagonal = jnp.exp(jax.random.uniform(diag_key, rough_part.shape[:-1], jnp.float32, math.log(low_value), math.log(high_value)))
    row_ids = lax.broadcasted_iota(jnp.int32, (matrix_order, matrix_order), 0)
    col_ids = lax.broadcasted_iota(jnp.int32, (matrix_order, matrix_order), 1)
    lower_part = jnp.where(row_ids > col_ids, rough_part * (1.0 / math.sqrt(matrix_order)), 0.0)
    return lower_part + jnp.where(row_ids == col_ids, diagonal[..., :, None], 0.0)


def draw_top_inverse(key, part):
    key = jax.random.fold_in(key, 11)
    first_key, second_key = jax.random.split(key)
    rough_part = jax.random.normal(second_key, (S, S), jnp.float32)
    return lower_factor(first_key, rough_part, 0.4, 4.0)


def draw_child_inverse(key, part):
    key = jax.random.fold_in(key, 23)
    first_key, second_key = jax.random.split(key)
    rough_part = jax.random.normal(second_key, (KIDS, C, C), jnp.float32)
    return lower_factor(first_key, rough_part, 0.5, 3.0)


def draw_ancestors(key, part):
    key = jax.random.fold_in(key, 5)
    member_keys = jax.random.split(key, KIDS)

    def one_list(member_key):
        inner_rows = jax.random.permutation(member_key, S - 2)[:R - 2].astype(jnp.int32) + 1
        ends = jnp.array([0, S - 1], jnp.int32)
        return jnp.sort(jnp.concatenate([ends, inner_rows]))
    return jax.vmap(one_list)(member_keys).astype(jnp.int32)


def block_scale(key, dims, pieces, smallest, largest):
    def one(position, blocks):
        steps = jax.random.uniform(jax.random.fold_in(jax.random.fold_in(key, 6), position), (blocks,), jnp.float32, smallest / len(pieces), largest / len(pieces))
        return jnp.repeat(jnp.exp(steps), dims[position] // blocks).reshape((-1,) + (1,) * (len(dims) - position - 1))

    loudness = one(*pieces[0])
    for cut in pieces[1:]:
        loudness = loudness * one(*cut)
    return loudness


def normal_values(key, shape, width, bound, cuts=(), dtype=jnp.bfloat16):
    factor_of = block_scale(key, shape, cuts, -0.22, 0.18) if cuts else 1.0
    drawn = jax.random.normal(key, shape, jnp.float32) * width * factor_of
    return jnp.minimum(jnp.maximum(drawn, -bound), bound).astype(dtype)


def setup_inputs(seed: int = 0) -> dict:
    keys = jax.random.split(jax.random.key(seed), 5)
    top_inverse = draw_top_inverse(jax.random.fold_in(keys[4], 71), 0)
    ancestors = draw_ancestors(jax.random.fold_in(keys[4], 71), 0)
    child_panel = normal_values(keys[2], (KIDS, R, C), C ** -0.5, 0.109375, ((0, 2), (1, 8), (2, 8)), jnp.float32)
    child_inverse = draw_child_inverse(jax.random.fold_in(keys[4], 71), 0)
    return dict(top_inverse=top_inverse, ancestors=ancestors, child_panel=child_panel, child_inverse=child_inverse)


def product(first_matrix, second_matrix):
    return jnp.dot(first_matrix, second_matrix, precision=lax.Precision.HIGHEST, preferred_element_type=jnp.float32)


def reference(top_inverse, ancestors, child_panel, child_inverse):
    top_block = product(top_inverse.T, top_inverse)
    crosses = []
    blocks = []
    for member in range(KIDS):
        index_list = ancestors[member].astype(jnp.int32)
        ancestor_cov = top_block[index_list][:, index_list]
        factor_prod = product(child_panel[member], child_inverse[member])
        cross = -product(ancestor_cov, factor_prod)
        block = product(child_inverse[member].T, child_inverse[member]) - product(factor_prod.T, cross)
        crosses.append(cross)
        blocks.append(block)
    return top_block, jnp.stack(crosses), jnp.stack(blocks)
```

```python
import jax
import jax.numpy as jnp
from jax import lax
from jax.sharding import Mesh, PartitionSpec as P

HIGH = lax.Precision.HIGH
AXES = ("sub", "x", "zl", "y", "core")
SIZES = (2, 4, 2, 4, 2)
ROWS = ("sub", "x", "zl")
COLS = ("y", "core")


def dot(a, b, da, db):
    return lax.dot_general(
        a, b, (((da,), (db,)), ((), ())), precision=HIGH, preferred_element_type=jnp.float32
    )


def along(value, axis, step):
    return lax.ppermute(value, axis, [(i, (i + step) % 4) for i in range(4)])


def along_z(value, step):
    return lax.ppermute(value, ("sub", "zl"), [(i, (i + step) % 4) for i in range(4)])


def other(value, axis):
    return lax.ppermute(value, axis, [(0, 1), (1, 0)])


def pick(stack, index):
    return lax.dynamic_index_in_dim(stack, index, 0, keepdims=False)


def on_device(top_inverse, ancestors, child_panel, child_inverse):
    sub, x, zl, y, core = (lax.axis_index(a) for a in AXES)
    z = 2 * sub + zl
    panel = child_panel[0]
    inverse = child_inverse[0]
    rows, width = panel.shape
    stripe, block = top_inverse.shape
    order = ancestors.shape[1]

    mine = top_inverse.T
    held = [mine] + [along(mine, "y", e) for e in (1, 3, 2)]
    held = jnp.stack([held[0], held[1], held[3], held[2]])
    across = other(held, "core")
    inverse_x = [inverse] + [along(inverse, "x", d) for d in (1, 2, 3)]
    top_z = [top_inverse] + [along_z(top_inverse, d) for d in (1, 2, 3)]
    flip = [(2 * a + c, 2 * (1 - a) + (1 - c)) for a in (0, 1) for c in (0, 1) if a != c]
    flipped = lax.ppermute(panel, ("zl", "core"), flip)
    panel_here = jnp.where(core == zl, panel, flipped)
    panels = lax.all_gather(panel_here, COLS, axis=0)
    inverses = lax.all_gather(inverse, COLS, axis=0)

    wanted = pick(ancestors, core)
    owner = wanted // block
    place = (y - owner // 2) % 4 + jnp.where(owner % 2 == core, 0, 4)
    both = jnp.concatenate([held, across]).reshape(8 * block, stripe)
    chosen = jnp.take(both, place * block + wanted % block, axis=0, mode="clip")
    share = order // 4
    own_cols = lax.dynamic_slice_in_dim(chosen, y * share, share, 0)
    part = dot(chosen, own_cols, 1, 1).reshape(order, 2, share // 2)
    part = part.transpose(1, 0, 2)
    kept, sent = pick(part, core), pick(part, 1 - core)
    came = other(sent, "core")
    first = core == 0
    part = jnp.stack([jnp.where(first, kept, came), jnp.where(first, came, kept)])
    part = part.reshape(16, rows, share // 2)
    cov = lax.all_to_all(part, ROWS, 0, 0).sum(0)
    cov_y = [cov] + [along(cov, "y", e) for e in (1, 2, 3)]
    cov_y = jnp.stack(cov_y)
    cov_all = jnp.concatenate([cov_y, other(cov_y, "core")])

    right = jnp.concatenate(inverse_x, 0)
    left = jnp.concatenate(
        [pick(panels.reshape(4, 2, rows, width), (x - d) % 4) for d in range(4)], 2
    ).reshape(2 * rows, 4 * width)
    factor_part = dot(left, right, 1, 0).reshape(2, rows, width)
    factor = pick(factor_part, zl) + other(pick(factor_part, 1 - zl), "zl")
    factors = lax.all_gather(factor, COLS, axis=0)
    factor_x = jnp.concatenate([factor] + [along(factor, "x", d) for d in (1, 2, 3)], 0)
    factor_col = jnp.concatenate([factor_x, other(factor_x, "zl")], 0)

    def cov_block(d, parity):
        at = (y - (x - d)) % 4 + jnp.where(parity == core, 0, 4)
        return pick(cov_all, at)

    cov_row = jnp.concatenate(
        [cov_block(d, parity) for parity in (zl, 1 - zl) for d in range(4)], 1
    )
    cross = -dot(cov_row, factor_col, 1, 0)
    cross_x = jnp.concatenate([cross] + [along(cross, "x", d) for d in (1, 2, 3)], 0)

    def panels_of(stack):
        own = [pick(stack, 2 * x + core)]
        own += [along(pick(stack, 2 * ((x + d) % 4) + core), "x", d) for d in (1, 2, 3)]
        there = [pick(stack, 2 * x + 1 - core)]
        there += [other(v, "core") for v in own[1:]]
        return jnp.concatenate(own, 0), jnp.concatenate(there, 0)

    same = core == zl
    left_own, left_there = panels_of(inverses)
    gram_own, gram_there = dot(left_own, right, 0, 0), dot(left_there, right, 0, 0)
    up_own, up_there = panels_of(factors)
    block_own = gram_own - dot(up_own, cross_x, 0, 0)
    block_there = gram_there - dot(up_there, cross_x, 0, 0)
    child_block = jnp.where(same, block_own, block_there) + other(
        jnp.where(same, block_there, block_own), "zl"
    )

    halves = held.reshape(4, 2, block // 2, stripe)

    def rows_for(source, target):
        t_sub, t_zl = target // 2, target % 2
        return jnp.concatenate(
            [pick(pick(source, (y - 2 * t_sub - h) % 4), t_zl) for h in (0, 1)], 0
        )

    own = [rows_for(halves, z)] + [along_z(rows_for(halves, (z + d) % 4), d) for d in (1, 2, 3)]
    there = [rows_for(across.reshape(halves.shape), z)] + [other(v, "core") for v in own[1:]]
    top_right = jnp.concatenate(top_z, 0)
    own = dot(jnp.concatenate(own, 1), top_right, 1, 0).reshape(2, stripe, block)
    there = dot(jnp.concatenate(there, 1), top_right, 1, 0).reshape(2, stripe, block)
    top_part = jnp.stack([jnp.where(first, own, there), jnp.where(first, there, own)], 1)
    top_block = lax.all_to_all(top_part.reshape(4, stripe, block), "x", 0, 0).sum(0)
    return top_block, cross[None], child_block[None]


def solution(mesh):
    fine = Mesh(mesh.devices.reshape(SIZES), AXES)
    child = P("sub", ("x", "zl"), COLS)
    top = P(ROWS, COLS)
    return jax.shard_map(
        on_device,
        mesh=fine,
        in_specs=(top, P(), child, child),
        out_specs=(top, child, child),
        check_vma=False,
    )
```

```python
import jax
import jax.numpy as jnp
from jax import lax
from jax.experimental import pallas as pl
from jax.experimental.pallas import tpu as pltpu
from jax.sharding import Mesh, PartitionSpec as P

AXES = ("sub", "x", "zl", "y", "core")
SIZES = (2, 4, 2, 4, 2)
ROWS = ("sub", "x", "zl")
COLS = ("y", "core")
F32 = jnp.float32
VMEM_BYTES = 60 * 2**20


def along(value, axis, step):
    return lax.ppermute(value, axis, [(i, (i + step) % 4) for i in range(4)])


def along_z(value, step):
    return lax.ppermute(value, ("sub", "zl"), [(i, (i + step) % 4) for i in range(4)])


def other(value, axis):
    return lax.ppermute(value, axis, [(0, 1), (1, 0)])


def parts(value):
    high = value.astype(jnp.bfloat16)
    return high, (value - high.astype(F32)).astype(jnp.bfloat16)


def product(a, b, da, db):
    a_high, a_low = parts(a)
    b_high, b_low = parts(b)

    def one(first, second):
        return lax.dot_general(
            first, second, (((da,), (db,)), ((), ())), preferred_element_type=F32
        )

    return one(a_high, b_high) + (one(a_high, b_low) + one(a_low, b_high))


def fetch(pairs, sems):
    copies = [pltpu.make_async_copy(s, d, sems.at[i]) for i, (s, d) in enumerate(pairs)]
    for copy in copies:
        copy.start()
    return copies


def finish(copies):
    for copy in copies:
        copy.wait()


def call(kernel, where, inputs, outs, scratch, copies, indices=(), direct=()):
    n_in = len(inputs)
    smem = pl.BlockSpec(memory_space=pltpu.SMEM)
    anywhere = pl.BlockSpec(memory_space=pl.ANY)
    vmem = pl.BlockSpec(memory_space=pltpu.VMEM)
    return pl.pallas_call(
        kernel,
        out_shape=list(outs),
        in_specs=[smem] * (1 + len(indices)) + [anywhere] * n_in,
        out_specs=[anywhere if i in direct else vmem for i in range(len(outs))],
        scratch_shapes=list(scratch) + [pltpu.SemaphoreType.DMA((copies,))],
        compiler_params=pltpu.CompilerParams(vmem_limit_bytes=VMEM_BYTES),
        cost_estimate=pl.CostEstimate(flops=1, bytes_accessed=1, transcendentals=0),
    )(where, *indices, *inputs)


def shape(*dims):
    return jax.ShapeDtypeStruct(dims, F32)


def spot(where):
    return [where[i] for i in range(5)]


def select_kernel(where, index, *refs):
    pieces, (out, *sent), (stripe, picked, sems) = refs[:8], refs[8:14], refs[14:]
    sub, x, zl, y, core = spot(where)
    size, depth = pieces[0].shape
    finish(fetch([(p, stripe.at[pl.ds(i * size, size)]) for i, p in enumerate(pieces)], sems))
    half = size // 2
    pairs = []
    for i in range(5):
        target = (2 * sub + zl + i % 4) % 4
        for h in range(2):
            place = (y - 2 * (target // 2) - h + 8) % 4 + (4 if i == 4 else 0)
            row = pl.multiple_of(place * size + (target % 2) * half, half)
            pairs.append((stripe.at[pl.ds(row, half)], sent[i].at[pl.ds(h * half, half)]))
    copies = fetch(pairs, sems)

    def eight(i, carry):
        for k in range(8):
            at = i * 8 + k
            picked[pl.ds(at, 1), :] = stripe[pl.ds(index[at], 1), :]
        return carry

    count = picked.shape[0]
    lax.fori_loop(0, count // 8, eight, 0)
    order, share = count // 2, out.shape[2]
    for child in range(2):
        left = picked[pl.ds(child * order, order), :]
        start = pl.multiple_of(child * order + (2 * y + core) * share, share)
        right = picked[pl.ds(start, share), :]
        block = product(left, right, 1, 1).reshape(order // share, share, share)
        out[pl.ds(child * (order // share), order // share)] = block
    finish(copies)


def cross_kernel(where, *refs):
    covs, factors, out, (held, right, sems) = refs[:8], refs[8:12], refs[12], refs[13:]
    sub, x, zl, y, core = spot(where)
    depth = right.shape[0] // 4
    pairs = [(c, held.at[i]) for i, c in enumerate(covs)]
    pairs += [(f, right.at[pl.ds(i * depth, depth)]) for i, f in enumerate(factors)]
    finish(fetch(pairs, sems))

    def block(i):
        return held[(y - x + i // 2 + 8) % 4 + jnp.where(core == i % 2, 0, 4)]

    out[...] = -product(jnp.concatenate([block(i) for i in range(8)], 1), right[...], 1, 0)


def factor_kernel(where, *refs):
    panels, inverses, out, (left, right, sems) = refs[:8], refs[8:12], refs[12], refs[13:]
    sub, x, zl, y, core = spot(where)
    pairs = [
        (p, left.at[(core + i // 4) % 2, (y - i % 4 + 4) % 4]) for i, p in enumerate(panels)
    ]
    pairs += [(v, right.at[(x - i + 4) % 4]) for i, v in enumerate(inverses)]
    finish(fetch(pairs, sems))
    both = jnp.concatenate(
        [jnp.concatenate([left[p, i] for i in range(4)], 1) for p in range(2)], 0
    )
    out[...] = product(both, right[...].reshape(both.shape[1], out.shape[1]), 1, 0)


def whole_kernel(where, *refs):
    mine, came, both, turned = refs
    total = mine[...] + came[...]
    both[...] = total
    rows = turned.shape[1]

    @pl.when(where[2] == 0)
    def _():
        turned[...] = total[:rows].T

    @pl.when(where[2] == 1)
    def _():
        turned[...] = total[rows:].T


def fetch_left(lefts, left, core, zl, y):
    mine = jnp.where(core == zl, 0, 1)
    return [(p, left.at[(mine + i // 4) % 2, (y - i % 4 + 4) % 4]) for i, p in enumerate(lefts)]


def gram_kernel(where, *refs):
    lefts, rights, (keep, send), (left, right, sems) = refs[:8], refs[8:12], refs[12:14], refs[14:]
    sub, x, zl, y, core = spot(where)
    pairs = fetch_left(lefts, left, core, zl, y)
    pairs += [(v, right.at[(x - i + 4) % 4]) for i, v in enumerate(rights)]
    finish(fetch(pairs, sems))
    depth = right.shape[0] * right.shape[1]
    for slot, out in ((1, send), (0, keep)):
        both = jnp.concatenate([left[slot, i] for i in range(4)], 1)
        out[...] = product(both, right[...].reshape(depth, right.shape[2]), 1, 0)


def update_kernel(where, *refs):
    keep_gram, send_gram, refs = refs[0], refs[1], refs[2:]
    lefts, rights, (keep, send), (left, right, sems) = refs[:8], refs[8:12], refs[12:14], refs[14:]
    sub, x, zl, y, core = spot(where)
    pairs = fetch_left(lefts, left, core, zl, y)
    pairs += [(v, right.at[(x - i + 4) % 4]) for i, v in enumerate(rights)]
    finish(fetch(pairs + [(keep_gram, keep), (send_gram, send)], sems))
    depth = right.shape[0] * right.shape[1]
    for slot, out in ((1, send), (0, keep)):
        both = jnp.concatenate([left[slot, i] for i in range(4)], 1)
        out[...] = out[...] - product(both, right[...].reshape(depth, right.shape[2]), 1, 0)


def flip_kernel(value, out):
    out[...] = value[...].T


def top_kernel(where, *refs):
    lefts, rights, out, (left, right, sems) = refs[:8], refs[8], refs[9], refs[10:]
    sub, x, zl, y, core = spot(where)
    depth = right.shape[0] // 4
    pairs = [(p, left.at[(core + i // 4) % 2, i % 4]) for i, p in enumerate(lefts)]
    for i in range(4):
        pairs.append((rights.at[(2 * sub + zl - i + 4) % 4], right.at[pl.ds(i * depth, depth)]))
    finish(fetch(pairs, sems))
    rows = out.shape[1]
    for parity in range(2):
        both = jnp.concatenate([left[parity, i] for i in range(4)], 1)
        total = product(both, right[...], 1, 0)
        for h in range(2):
            out[2 * h + parity] = total[h * rows : (h + 1) * rows]


def after(value, *first):
    return lax.optimization_barrier((value, *first))[0]


def on_device(top_inverse, ancestors, child_panel, child_inverse):
    sub, x, zl, y, core = (lax.axis_index(a) for a in AXES)
    where = jnp.stack([sub, x, zl, y, core]).astype(jnp.int32)
    panel = child_panel[0]
    inverse = child_inverse[0]
    rows, width = panel.shape
    stripe, block = top_inverse.shape
    order = ancestors.shape[1]
    share = order // 8

    def vmem(*dims):
        return pltpu.VMEM(dims, F32)

    def flipped(value):
        return pl.pallas_call(
            flip_kernel,
            out_shape=shape(value.shape[1], value.shape[0]),
            cost_estimate=pl.CostEstimate(flops=1, bytes_accessed=1, transcendentals=0),
        )(value)

    def swap_xy(value):
        pairs = [(4 * a + b, 4 * b + a) for a in range(4) for b in range(4)]
        return lax.ppermute(value, ("x", "y"), pairs)

    def over_y(value):
        return [value] + [along(value, "y", e) for e in (1, 2, 3)]

    def both_cores(values):
        return values + [other(v, "core") for v in values]

    stripes = over_y(flipped(top_inverse))
    flip = [(2 * a + c, 2 * (1 - a) + (1 - c)) for a in (0, 1) for c in (0, 1) if a != c]
    panel = jnp.where(core == zl, panel, lax.ppermute(panel, ("zl", "core"), flip))
    inverse_x = {0: inverse} | {d: along(inverse, "x", d) for d in (1, 3)}
    top_z = lax.all_gather(top_inverse, ("sub", "zl"), axis=0)
    inverse_t = flipped(inverse)
    stripes, panel, inverse_t, inverse = lax.optimization_barrier(
        (stripes, panel, inverse_t, inverse)
    )

    panels = over_y(panel)
    inverse_x[2] = along(inverse, "x", 2)
    inverse_x = [inverse_x[d] for d in range(4)]
    inverse_t = swap_xy(inverse_t)
    owner = ancestors // block
    place = (y - owner // 2) % 4 + jnp.where(owner % 2 == core, 0, 4)
    index = (place * block + ancestors % block).reshape(-1)
    part, own0, own1, own2, own3, there0 = call(
        select_kernel, where, both_cores(stripes),
        [shape(16, share, share)] + [shape(block, stripe)] * 5,
        [vmem(8 * block, stripe), vmem(2 * order, stripe)], 10, (index,), (1, 2, 3, 4, 5),
    )
    part, own1, own2, own3, panels, inverse_x = lax.optimization_barrier(
        (part, own1, own2, own3, panels, inverse_x)
    )

    cov = lax.all_to_all(part, ROWS, 0, 0).sum(0)
    (factor_part,) = call(
        factor_kernel, where, both_cores(panels) + inverse_x,
        [shape(2 * rows, width)], [vmem(2, 4, rows, width), vmem(4, width, width)], 12,
    )
    factor, factor_t = pl.pallas_call(
        whole_kernel,
        out_shape=[shape(2 * rows, width), shape(width, rows)],
        in_specs=[pl.BlockSpec(memory_space=pltpu.SMEM)]
        + [pl.BlockSpec(memory_space=pltpu.VMEM)] * 2,
        out_specs=[pl.BlockSpec(memory_space=pltpu.VMEM)] * 2,
        compiler_params=pltpu.CompilerParams(vmem_limit_bytes=VMEM_BYTES),
        cost_estimate=pl.CostEstimate(flops=1, bytes_accessed=1, transcendentals=0),
    )(where, factor_part, other(factor_part, "zl"))
    inverse_columns = over_y(inverse_t)
    cov, factor, factor_t, inverse_columns = lax.optimization_barrier(
        (cov, factor, factor_t, inverse_columns)
    )

    factor_x = [factor] + [along(factor, "x", d) for d in (1, 2, 3)]
    cov_y = over_y(cov)
    (cross,) = call(
        cross_kernel, where, both_cores(cov_y) + factor_x, [shape(rows, width)],
        [vmem(8, rows, share), vmem(8 * rows, width)], 12,
    )
    own = [along_z(after(v, *cov_y), d + 1) for d, v in enumerate((own1, own2, own3))]
    factor_t = swap_xy(after(factor_t, factor_x[1], factor_x[2], factor_x[3]))
    cross, inverse_columns = lax.optimization_barrier((cross, inverse_columns))

    cross_x = [cross] + [along(cross, "x", d) for d in (1, 2, 3)]
    factor_columns = over_y(factor_t)
    there = [there0] + [other(v, "core") for v in own]
    (top_part,) = call(
        top_kernel, where, [own0] + own + there + [top_z], [shape(4, stripe, block)],
        [vmem(2, 4, block, stripe), vmem(4 * stripe, block)], 12,
    )
    grams = call(
        gram_kernel, where, both_cores(inverse_columns) + inverse_x, [shape(width, width)] * 2,
        [vmem(2, 4, width, width), vmem(4, width, width)], 12,
    )
    grams, cross_x, factor_columns = lax.optimization_barrier((grams, cross_x, factor_columns))

    block_keep, block_send = call(
        update_kernel, where, list(grams) + both_cores(factor_columns) + cross_x,
        [shape(width, width)] * 2, [vmem(2, 4, width, rows), vmem(4, rows, width)], 14,
    )
    child_block = block_keep + other(block_send, "zl")
    top_block = lax.all_to_all(after(top_part, *cross_x[1:]), "x", 0, 0).sum(0)
    return top_block, cross[None], child_block[None]


def solution(mesh):
    fine = Mesh(mesh.devices.reshape(SIZES), AXES)
    child = P("sub", ("x", "zl"), COLS)
    top = P(ROWS, COLS)
    return jax.shard_map(
        on_device,
        mesh=fine,
        in_specs=(top, P(), child, child),
        out_specs=(top, child, child),
        check_vma=False,
    )
```

```python
import jax
import jax.numpy as jnp
from jax import lax
from jax.experimental import pallas as pl
from jax.experimental.pallas import tpu as pltpu
from jax.sharding import Mesh, PartitionSpec as P

AXES = ("sub", "x", "zl", "y", "core")
SIZES = (2, 4, 2, 4, 2)
ROWS = ("sub", "x", "zl")
COLS = ("y", "core")
F32 = jnp.float32
VMEM_BYTES = 60 * 2**20


def along(value, axis, step):
    return lax.ppermute(value, axis, [(i, (i + step) % 4) for i in range(4)])


def along_z(value, step):
    return lax.ppermute(value, ("sub", "zl"), [(i, (i + step) % 4) for i in range(4)])


def other(value, axis):
    return lax.ppermute(value, axis, [(0, 1), (1, 0)])


def parts(value):
    high = value.astype(jnp.bfloat16)
    return high, (value - high.astype(F32)).astype(jnp.bfloat16)


def product(a, b, da, db):
    a_high, a_low = parts(a)
    b_high, b_low = parts(b)

    def one(first, second):
        return lax.dot_general(
            first, second, (((da,), (db,)), ((), ())), preferred_element_type=F32
        )

    return one(a_high, b_high) + (one(a_high, b_low) + one(a_low, b_high))


def fetch(pairs, sems):
    copies = [pltpu.make_async_copy(s, d, sems.at[i]) for i, (s, d) in enumerate(pairs)]
    for copy in copies:
        copy.start()
    return copies


def finish(copies):
    for copy in copies:
        copy.wait()


def call(kernel, where, inputs, outs, scratch, copies, indices=(), direct=()):
    n_in = len(inputs)
    smem = pl.BlockSpec(memory_space=pltpu.SMEM)
    anywhere = pl.BlockSpec(memory_space=pl.ANY)
    vmem = pl.BlockSpec(memory_space=pltpu.VMEM)
    return pl.pallas_call(
        kernel,
        out_shape=list(outs),
        in_specs=[smem] * (1 + len(indices)) + [anywhere] * n_in,
        out_specs=[anywhere if i in direct else vmem for i in range(len(outs))],
        scratch_shapes=list(scratch) + [pltpu.SemaphoreType.DMA((copies,))],
        compiler_params=pltpu.CompilerParams(vmem_limit_bytes=VMEM_BYTES),
        cost_estimate=pl.CostEstimate(flops=1, bytes_accessed=1, transcendentals=0),
    )(where, *indices, *inputs)


def shape(*dims):
    return jax.ShapeDtypeStruct(dims, F32)


def spot(where):
    return [where[i] for i in range(5)]


def select_kernel(where, index, *refs):
    pieces, (out, *sent), (stripe, picked, sems) = refs[:8], refs[8:14], refs[14:]
    sub, x, zl, y, core = spot(where)
    size, depth = pieces[0].shape
    finish(fetch([(p, stripe.at[pl.ds(i * size, size)]) for i, p in enumerate(pieces)], sems))
    half = size // 2
    pairs = []
    for i in range(5):
        target = (2 * sub + zl + i % 4) % 4
        for h in range(2):
            place = (y - 2 * (target // 2) - h + 8) % 4 + (4 if i == 4 else 0)
            row = pl.multiple_of(place * size + (target % 2) * half, half)
            pairs.append((stripe.at[pl.ds(row, half)], sent[i].at[pl.ds(h * half, half)]))
    copies = fetch(pairs, sems)

    def eight(i, carry):
        for k in range(8):
            at = i * 8 + k
            picked[pl.ds(at, 1), :] = stripe[pl.ds(index[at], 1), :]
        return carry

    count = picked.shape[0]
    lax.fori_loop(0, count // 8, eight, 0)
    order, share = count // 2, out.shape[2]
    for child in range(2):
        left = picked[pl.ds(child * order, order), :]
        start = pl.multiple_of(child * order + (2 * y + core) * share, share)
        right = picked[pl.ds(start, share), :]
        block = product(left, right, 1, 1).reshape(order // share, share, share)
        out[pl.ds(child * (order // share), order // share)] = block
    finish(copies)


def cross_kernel(where, *refs):
    covs, factors, mine, out, sent = refs[:8], refs[8:12], refs[12:16], refs[16], refs[17:21]
    held, right, turned, sems = refs[21:]
    sub, x, zl, y, core = spot(where)
    depth = right.shape[0] // 4
    pairs = [(c, held.at[i]) for i, c in enumerate(covs)]
    pairs += [(f, right.at[pl.ds(i * depth, depth)]) for i, f in enumerate(factors)]
    pairs += [(p, turned.at[(y - x - e + 8) % 4]) for e, p in enumerate(mine)]
    finish(fetch(pairs, sems))

    def block(i):
        return held[(y - x + i // 2 + 8) % 4 + jnp.where(core == i % 2, 0, 4)]

    cross = -product(jnp.concatenate([block(i) for i in range(8)], 1), right[...], 1, 0)
    out[...] = cross
    rows = out.shape[0]
    for d in range(4):
        sent[d][:rows] = cross
        sent[d][rows:] = turned[d]


def factor_kernel(where, *refs):
    panels, inverses, out, (left, right, sems) = refs[:8], refs[8:12], refs[12], refs[13:]
    sub, x, zl, y, core = spot(where)
    pairs = [
        (p, left.at[(core + i // 4) % 2, (y - i % 4 + 4) % 4]) for i, p in enumerate(panels)
    ]
    pairs += [(v, right.at[(x - i + 4) % 4]) for i, v in enumerate(inverses)]
    finish(fetch(pairs, sems))
    both = jnp.concatenate(
        [jnp.concatenate([left[p, i] for i in range(4)], 1) for p in range(2)], 0
    )
    out[...] = product(both, right[...].reshape(both.shape[1], out.shape[1]), 1, 0)


def whole_kernel(where, mine, came, both, own):
    total = mine[...] + came[...]
    both[...] = total
    rows = own.shape[0]

    @pl.when(where[2] == 0)
    def _():
        own[...] = total[:rows]

    @pl.when(where[2] == 1)
    def _():
        own[...] = total[rows:]


def fetch_left(lefts, left, core, zl, at):
    mine = jnp.where(core == zl, 0, 1)
    return [(p, left.at[(mine + i // 4) % 2, (at - i % 4 + 4) % 4]) for i, p in enumerate(lefts)]


def gram_kernel(where, *refs):
    lefts, rights, (keep, send), (left, right, sems) = refs[:8], refs[8:12], refs[12:14], refs[14:]
    sub, x, zl, y, core = spot(where)
    pairs = fetch_left(lefts, left, core, zl, x)
    pairs += [(v, right.at[(x - i + 4) % 4]) for i, v in enumerate(rights)]
    finish(fetch(pairs, sems))
    depth = right.shape[0] * right.shape[1]
    for slot, out in ((1, send), (0, keep)):
        both = jnp.concatenate([left[slot, i] for i in range(4)], 1)
        out[...] = product(both, right[...].reshape(depth, right.shape[2]), 1, 0)


def update_kernel(where, *refs):
    keep_gram, send_gram, near, far = refs[0], refs[1], refs[2:6], refs[6:10]
    keep, send, left, right, sems = refs[10:]
    sub, x, zl, y, core = spot(where)
    mine = jnp.where(core == zl, 0, 1)
    rows = right.shape[1]
    pairs = [(keep_gram, keep), (send_gram, send)]
    for d in range(4):
        place = (x - d + 4) % 4
        pairs.append((near[d].at[pl.ds(0, rows)], right.at[place]))
        pairs.append((near[d].at[pl.ds(rows, rows)], left.at[mine, place]))
        pairs.append((far[d].at[pl.ds(rows, rows)], left.at[1 - mine, place]))
    finish(fetch(pairs, sems))
    straight = right[...].reshape(4 * rows, right.shape[2])
    for slot, out in ((1, send), (0, keep)):
        both = left[slot].reshape(4 * rows, left.shape[3])
        out[...] = out[...] - product(both, straight, 0, 0)


def turn_kernel(where, *refs):
    stack, outs, (held, sems) = refs[0], refs[1:5], refs[5:]
    sub, x, zl, y, core = spot(where)
    finish(fetch([(stack.at[(x + d) % 4], held.at[d]) for d in range(4)], sems))
    finish(fetch([(held.at[d], outs[d]) for d in range(4)], sems))


def flip_kernel(value, out):
    out[...] = value[...].T


def top_kernel(where, *refs):
    lefts, rights, out, (left, right, sems) = refs[:8], refs[8], refs[9], refs[10:]
    sub, x, zl, y, core = spot(where)
    pairs = [
        (p, left.at[(core + i // 4) % 2, (2 * sub + zl - i % 4 + 4) % 4])
        for i, p in enumerate(lefts)
    ]
    finish(fetch(pairs + [(rights, right)], sems))
    rows = out.shape[1]
    for parity in range(2):
        both = jnp.concatenate([left[parity, i] for i in range(4)], 1)
        total = product(both, right[...].reshape(both.shape[1], out.shape[2]), 1, 0)
        for h in range(2):
            out[2 * h + parity] = total[h * rows : (h + 1) * rows]


def after(value, *first):
    return lax.optimization_barrier((value, *first))[0]


def on_device(top_inverse, ancestors, child_panel, child_inverse):
    sub, x, zl, y, core = (lax.axis_index(a) for a in AXES)
    where = jnp.stack([sub, x, zl, y, core]).astype(jnp.int32)
    panel = child_panel[0]
    inverse = child_inverse[0]
    rows, width = panel.shape
    stripe, block = top_inverse.shape
    order = ancestors.shape[1]
    share = order // 8

    def vmem(*dims):
        return pltpu.VMEM(dims, F32)

    def flipped(value):
        return pl.pallas_call(
            flip_kernel,
            out_shape=shape(value.shape[1], value.shape[0]),
            cost_estimate=pl.CostEstimate(flops=1, bytes_accessed=1, transcendentals=0),
        )(value)

    def over_y(value):
        return [value] + [along(value, "y", e) for e in (1, 2, 3)]

    def both_cores(values):
        return values + [other(v, "core") for v in values]

    stripes = over_y(flipped(top_inverse))
    flip = [(2 * a + c, 2 * (1 - a) + (1 - c)) for a in (0, 1) for c in (0, 1) if a != c]
    panel = jnp.where(core == zl, panel, lax.ppermute(panel, ("zl", "core"), flip))
    inverse_x = [inverse] + [along(inverse, "x", d) for d in (1, 2, 3)]
    inverse_t = flipped(inverse)
    top_z = lax.all_gather(top_inverse, ("sub", "zl"), axis=0)
    stripes, panel, inverse_x, inverse_t = lax.optimization_barrier(
        (stripes, panel, inverse_x, inverse_t)
    )

    inverse_y = lax.all_gather(inverse_t, "y", axis=0)
    panels = over_y(panel)
    owner = ancestors // block
    place = (y - owner // 2) % 4 + jnp.where(owner % 2 == core, 0, 4)
    index = (place * block + ancestors % block).reshape(-1)
    part, own0, own1, own2, own3, there0 = call(
        select_kernel, where, both_cores(stripes),
        [shape(16, share, share)] + [shape(block, stripe)] * 5,
        [vmem(8 * block, stripe), vmem(2 * order, stripe)], 10, (index,), (1, 2, 3, 4, 5),
    )
    part, own1, own2, own3, panels, top_z = lax.optimization_barrier(
        (part, own1, own2, own3, panels, top_z)
    )

    cov = lax.all_to_all(part, ROWS, 0, 0).sum(0)
    (factor_part,) = call(
        factor_kernel, where, both_cores(panels) + inverse_x,
        [shape(2 * rows, width)], [vmem(2, 4, rows, width), vmem(4, width, width)], 12,
    )
    turned = call(
        turn_kernel, where, [after(inverse_y, factor_part)], [shape(width, width)] * 4,
        [vmem(4, width, width)], 4, (), (0, 1, 2, 3),
    )
    inverse_columns = [turned[0]] + [along(turned[d], "x", d) for d in (1, 2, 3)]
    factor, factor_own = pl.pallas_call(
        whole_kernel,
        out_shape=[shape(2 * rows, width), shape(rows, width)],
        in_specs=[pl.BlockSpec(memory_space=pltpu.SMEM)]
        + [pl.BlockSpec(memory_space=pltpu.VMEM)] * 2,
        out_specs=[pl.BlockSpec(memory_space=pltpu.VMEM)] * 2,
        compiler_params=pltpu.CompilerParams(vmem_limit_bytes=VMEM_BYTES),
        cost_estimate=pl.CostEstimate(flops=1, bytes_accessed=1, transcendentals=0),
    )(where, factor_part, other(factor_part, "zl"))
    cov_y = over_y(cov)
    cov_y, factor, factor_own, own1, own2, own3, inverse_columns[0] = lax.optimization_barrier(
        (cov_y, factor, factor_own, own1, own2, own3, inverse_columns[0])
    )

    factor_x = [factor] + [along(factor, "x", d) for d in (1, 2, 3)]
    own = [own0] + [along_z(v, d + 1) for d, v in enumerate((own1, own2, own3))]
    factor_y = over_y(factor_own)
    grams = call(
        gram_kernel, where, both_cores(inverse_columns) + inverse_x, [shape(width, width)] * 2,
        [vmem(2, 4, width, width), vmem(4, width, width)], 12,
    )
    cov_y[0] = after(cov_y[0], grams[0])
    cross, *sent = call(
        cross_kernel, where, both_cores(cov_y) + factor_x + factor_y,
        [shape(rows, width)] + [shape(2 * rows, width)] * 4,
        [vmem(8, rows, share), vmem(8 * rows, width), vmem(4, rows, width)], 16,
    )
    cross, sent, grams, own = lax.optimization_barrier((cross, sent, grams, own))

    near = [sent[0]] + [along(sent[d], "x", d) for d in (1, 2, 3)]
    there = [there0] + [other(v, "core") for v in own[1:]]
    (top_part,) = call(
        top_kernel, where, own + there + [top_z], [shape(4, stripe, block)],
        [vmem(2, 4, block, stripe), vmem(4, stripe, block)], 9,
    )
    near, top_part = lax.optimization_barrier((near, top_part))

    far = [other(v, "core") for v in near]
    block_keep, block_send = call(
        update_kernel, where, list(grams) + near + far, [shape(width, width)] * 2,
        [vmem(2, 4, rows, width), vmem(4, rows, width)], 14,
    )
    child_block = block_keep + other(block_send, "zl")
    top_block = lax.all_to_all(top_part, "x", 0, 0).sum(0)
    return top_block, cross[None], child_block[None]


def solution(mesh):
    fine = Mesh(mesh.devices.reshape(SIZES), AXES)
    child = P("sub", ("x", "zl"), COLS)
    top = P(ROWS, COLS)
    return jax.shard_map(
        on_device,
        mesh=fine,
        in_specs=(top, P(), child, child),
        out_specs=(top, child, child),
        check_vma=False,
    )
```

```python
import jax
import jax.numpy as jnp
from jax import lax
from jax.experimental import pallas as pl
from jax.experimental.pallas import tpu as pltpu
from jax.sharding import Mesh, PartitionSpec as P

AXES = ("sub", "x", "zl", "y", "core")
SIZES = (2, 4, 2, 4, 2)
ROWS = ("sub", "x", "zl")
COLS = ("y", "core")
F32 = jnp.float32
VMEM_BYTES = 60 * 2**20


def along(value, axis, step):
    return lax.ppermute(value, axis, [(i, (i + step) % 4) for i in range(4)])


def along_z(value, step):
    return lax.ppermute(value, ("sub", "zl"), [(i, (i + step) % 4) for i in range(4)])


def other(value, axis):
    return lax.ppermute(value, axis, [(0, 1), (1, 0)])


def parts(value):
    high = value.astype(jnp.bfloat16)
    return high, (value - high.astype(F32)).astype(jnp.bfloat16)


def product(a, b, da, db):
    a_high, a_low = parts(a)
    b_high, b_low = parts(b)

    def one(first, second):
        return lax.dot_general(
            first, second, (((da,), (db,)), ((), ())), preferred_element_type=F32
        )

    return one(a_high, b_high) + (one(a_high, b_low) + one(a_low, b_high))


def fetch(pairs, sems):
    copies = [pltpu.make_async_copy(s, d, sems.at[i]) for i, (s, d) in enumerate(pairs)]
    for copy in copies:
        copy.start()
    return copies


def finish(copies):
    for copy in copies:
        copy.wait()


def call(kernel, where, inputs, outs, scratch, copies, indices=(), direct=()):
    n_in = len(inputs)
    smem = pl.BlockSpec(memory_space=pltpu.SMEM)
    anywhere = pl.BlockSpec(memory_space=pl.ANY)
    vmem = pl.BlockSpec(memory_space=pltpu.VMEM)
    return pl.pallas_call(
        kernel,
        out_shape=list(outs),
        in_specs=[smem] * (1 + len(indices)) + [anywhere] * n_in,
        out_specs=[anywhere if i in direct else vmem for i in range(len(outs))],
        scratch_shapes=list(scratch) + [pltpu.SemaphoreType.DMA((copies,))],
        compiler_params=pltpu.CompilerParams(vmem_limit_bytes=VMEM_BYTES),
        cost_estimate=pl.CostEstimate(flops=1, bytes_accessed=1, transcendentals=0),
    )(where, *indices, *inputs)


def shape(*dims):
    return jax.ShapeDtypeStruct(dims, F32)


def spot(where):
    return [where[i] for i in range(5)]


def select_kernel(where, index, *refs):
    pieces, (out, *sent), (stripe, picked, sems) = refs[:8], refs[8:14], refs[14:]
    sub, x, zl, y, core = spot(where)
    size, depth = pieces[0].shape
    finish(fetch([(p, stripe.at[pl.ds(i * size, size)]) for i, p in enumerate(pieces)], sems))
    half = size // 2
    pairs = []
    for i in range(5):
        target = (2 * sub + zl + i % 4) % 4
        for h in range(2):
            place = (y - 2 * (target // 2) - h + 8) % 4 + (4 if i == 4 else 0)
            row = pl.multiple_of(place * size + (target % 2) * half, half)
            pairs.append((stripe.at[pl.ds(row, half)], sent[i].at[pl.ds(h * half, half)]))
    copies = fetch(pairs, sems)

    def some(i, carry):
        found = [stripe[pl.ds(index[i * 32 + k], 1), :] for k in range(32)]
        for k in range(32):
            picked[pl.ds(i * 32 + k, 1), :] = found[k]
        return carry

    count = picked.shape[0]
    lax.fori_loop(0, count // 32, some, 0)
    order, share = count // 2, out.shape[2]
    for child in range(2):
        left = picked[pl.ds(child * order, order), :]
        start = pl.multiple_of(child * order + (2 * y + core) * share, share)
        right = picked[pl.ds(start, share), :]
        block = product(left, right, 1, 1).reshape(order // share, share, share)
        out[pl.ds(child * (order // share), order // share)] = block
    finish(copies)


def cross_kernel(where, *refs):
    covs, factors, mine, out, sent = refs[:8], refs[8:12], refs[12:16], refs[16], refs[17:21]
    held, right, turned, sems = refs[21:]
    sub, x, zl, y, core = spot(where)
    depth = right.shape[0] // 4
    pairs = [(c, held.at[i]) for i, c in enumerate(covs)]
    pairs += [(f, right.at[pl.ds(i * depth, depth)]) for i, f in enumerate(factors)]
    pairs += [(p, turned.at[(y - x - e + 8) % 4]) for e, p in enumerate(mine)]
    finish(fetch(pairs, sems))

    def block(i):
        return held[(y - x + i // 2 + 8) % 4 + jnp.where(core == i % 2, 0, 4)]

    cross = -product(jnp.concatenate([block(i) for i in range(8)], 1), right[...], 1, 0)
    out[...] = cross
    rows = out.shape[0]
    for d in range(4):
        sent[d][:rows] = cross
        sent[d][rows:] = turned[d]


def factor_kernel(where, *refs):
    panels, inverses, out, (left, right, sems) = refs[:8], refs[8:12], refs[12], refs[13:]
    sub, x, zl, y, core = spot(where)
    pairs = [
        (p, left.at[(core + i // 4) % 2, (y - i % 4 + 4) % 4]) for i, p in enumerate(panels)
    ]
    pairs += [(v, right.at[(x - i + 4) % 4]) for i, v in enumerate(inverses)]
    finish(fetch(pairs, sems))
    both = jnp.concatenate(
        [jnp.concatenate([left[p, i] for i in range(4)], 1) for p in range(2)], 0
    )
    out[...] = product(both, right[...].reshape(both.shape[1], out.shape[1]), 1, 0)


def whole_kernel(where, mine, came, both, own):
    total = mine[...] + came[...]
    both[...] = total
    rows = own.shape[0]

    @pl.when(where[2] == 0)
    def _():
        own[...] = total[:rows]

    @pl.when(where[2] == 1)
    def _():
        own[...] = total[rows:]


def fetch_left(lefts, left, core, zl, at):
    mine = jnp.where(core == zl, 0, 1)
    return [(p, left.at[(mine + i // 4) % 2, (at - i % 4 + 4) % 4]) for i, p in enumerate(lefts)]


def gram_kernel(where, *refs):
    lefts, rights, (keep, send), (left, right, sems) = refs[:8], refs[8:12], refs[12:14], refs[14:]
    sub, x, zl, y, core = spot(where)
    pairs = fetch_left(lefts, left, core, zl, x)
    pairs += [(v, right.at[(x - i + 4) % 4]) for i, v in enumerate(rights)]
    finish(fetch(pairs, sems))
    depth = right.shape[0] * right.shape[1]
    for slot, out in ((1, send), (0, keep)):
        both = jnp.concatenate([left[slot, i] for i in range(4)], 1)
        out[...] = product(both, right[...].reshape(depth, right.shape[2]), 1, 0)


def update_kernel(where, *refs):
    keep_gram, send_gram, near, far = refs[0], refs[1], refs[2:6], refs[6:10]
    keep, send, left, right, sems = refs[10:]
    sub, x, zl, y, core = spot(where)
    mine = jnp.where(core == zl, 0, 1)
    rows = right.shape[1]
    pairs = [(keep_gram, keep), (send_gram, send)]
    for d in range(4):
        place = (x - d + 4) % 4
        pairs.append((near[d].at[pl.ds(0, rows)], right.at[place]))
        pairs.append((near[d].at[pl.ds(rows, rows)], left.at[mine, place]))
        pairs.append((far[d].at[pl.ds(rows, rows)], left.at[1 - mine, place]))
    finish(fetch(pairs, sems))
    straight = right[...].reshape(4 * rows, right.shape[2])
    for slot, out in ((1, send), (0, keep)):
        both = left[slot].reshape(4 * rows, left.shape[3])
        out[...] = out[...] - product(both, straight, 0, 0)


def turn_kernel(where, *refs):
    stack, outs, (held, sems) = refs[0], refs[1:5], refs[5:]
    sub, x, zl, y, core = spot(where)
    finish(fetch([(stack.at[(x + d) % 4], held.at[d]) for d in range(4)], sems))
    finish(fetch([(held.at[d], outs[d]) for d in range(4)], sems))


def flip_kernel(value, out):
    out[...] = value[...].T


def top_kernel(where, *refs):
    lefts, rights, out, (left, right, sems) = refs[:8], refs[8], refs[9], refs[10:]
    sub, x, zl, y, core = spot(where)
    pairs = [
        (p, left.at[(core + i // 4) % 2, (2 * sub + zl - i % 4 + 4) % 4])
        for i, p in enumerate(lefts)
    ]
    finish(fetch(pairs + [(rights, right)], sems))
    rows = out.shape[1]
    for parity in range(2):
        both = jnp.concatenate([left[parity, i] for i in range(4)], 1)
        total = product(both, right[...].reshape(both.shape[1], out.shape[2]), 1, 0)
        for h in range(2):
            out[2 * h + parity] = total[h * rows : (h + 1) * rows]


def after(value, *first):
    return lax.optimization_barrier((value, *first))[0]


def on_device(top_inverse, ancestors, child_panel, child_inverse):
    sub, x, zl, y, core = (lax.axis_index(a) for a in AXES)
    where = jnp.stack([sub, x, zl, y, core]).astype(jnp.int32)
    panel = child_panel[0]
    inverse = child_inverse[0]
    rows, width = panel.shape
    stripe, block = top_inverse.shape
    order = ancestors.shape[1]
    share = order // 8

    def vmem(*dims):
        return pltpu.VMEM(dims, F32)

    def flipped(value):
        return pl.pallas_call(
            flip_kernel,
            out_shape=shape(value.shape[1], value.shape[0]),
            cost_estimate=pl.CostEstimate(flops=1, bytes_accessed=1, transcendentals=0),
        )(value)

    def over_y(value):
        return [value] + [along(value, "y", e) for e in (1, 2, 3)]

    def both_cores(values):
        return values + [other(v, "core") for v in values]

    stripes = over_y(flipped(top_inverse))
    flip = [(2 * a + c, 2 * (1 - a) + (1 - c)) for a in (0, 1) for c in (0, 1) if a != c]
    panel = jnp.where(core == zl, panel, lax.ppermute(panel, ("zl", "core"), flip))
    inverse_x = [inverse] + [along(inverse, "x", d) for d in (1, 2, 3)]
    inverse_t = flipped(inverse)
    top_z = lax.all_gather(top_inverse, ("sub", "zl"), axis=0)
    stripes, panel, inverse_x, inverse_t = lax.optimization_barrier(
        (stripes, panel, inverse_x, inverse_t)
    )

    inverse_y = lax.all_gather(inverse_t, "y", axis=0)
    panels = over_y(panel)
    owner = ancestors // block
    place = (y - owner // 2) % 4 + jnp.where(owner % 2 == core, 0, 4)
    index = (place * block + ancestors % block).reshape(-1)
    part, own0, own1, own2, own3, there0 = call(
        select_kernel, where, both_cores(stripes),
        [shape(16, share, share)] + [shape(block, stripe)] * 5,
        [vmem(8 * block, stripe), vmem(2 * order, stripe)], 10, (index,), (1, 2, 3, 4, 5),
    )
    part, own1, own2, own3, panels, top_z = lax.optimization_barrier(
        (part, own1, own2, own3, panels, top_z)
    )

    cov = lax.all_to_all(part, ROWS, 0, 0).sum(0)
    (factor_part,) = call(
        factor_kernel, where, both_cores(panels) + inverse_x,
        [shape(2 * rows, width)], [vmem(2, 4, rows, width), vmem(4, width, width)], 12,
    )
    turned = call(
        turn_kernel, where, [after(inverse_y, factor_part)], [shape(width, width)] * 4,
        [vmem(4, width, width)], 4, (), (0, 1, 2, 3),
    )
    inverse_columns = [turned[0]] + [along(turned[d], "x", d) for d in (1, 2, 3)]
    factor, factor_own = pl.pallas_call(
        whole_kernel,
        out_shape=[shape(2 * rows, width), shape(rows, width)],
        in_specs=[pl.BlockSpec(memory_space=pltpu.SMEM)]
        + [pl.BlockSpec(memory_space=pltpu.VMEM)] * 2,
        out_specs=[pl.BlockSpec(memory_space=pltpu.VMEM)] * 2,
        compiler_params=pltpu.CompilerParams(vmem_limit_bytes=VMEM_BYTES),
        cost_estimate=pl.CostEstimate(flops=1, bytes_accessed=1, transcendentals=0),
    )(where, factor_part, other(factor_part, "zl"))
    cov_y = over_y(cov)
    cov_y, factor, factor_own, own1, own2, own3, inverse_columns[0] = lax.optimization_barrier(
        (cov_y, factor, factor_own, own1, own2, own3, inverse_columns[0])
    )

    factor_x = [factor] + [along(factor, "x", d) for d in (1, 2, 3)]
    own = [own0] + [along_z(v, d + 1) for d, v in enumerate((own1, own2, own3))]
    factor_y = over_y(factor_own)
    grams = call(
        gram_kernel, where, both_cores(inverse_columns) + inverse_x, [shape(width, width)] * 2,
        [vmem(2, 4, width, width), vmem(4, width, width)], 12,
    )
    cov_y[0] = after(cov_y[0], grams[0])
    cross, *sent = call(
        cross_kernel, where, both_cores(cov_y) + factor_x + factor_y,
        [shape(rows, width)] + [shape(2 * rows, width)] * 4,
        [vmem(8, rows, share), vmem(8 * rows, width), vmem(4, rows, width)], 16,
    )
    cross, sent, grams, own = lax.optimization_barrier((cross, sent, grams, own))

    near = [sent[0]] + [along(sent[d], "x", d) for d in (1, 2, 3)]
    there = [there0] + [other(v, "core") for v in own[1:]]
    (top_part,) = call(
        top_kernel, where, own + there + [top_z], [shape(4, stripe, block)],
        [vmem(2, 4, block, stripe), vmem(4, stripe, block)], 9,
    )
    near, top_part = lax.optimization_barrier((near, top_part))

    far = [other(v, "core") for v in near]
    block_keep, block_send = call(
        update_kernel, where, list(grams) + near + far, [shape(width, width)] * 2,
        [vmem(2, 4, rows, width), vmem(4, rows, width)], 14,
    )
    child_block = block_keep + other(block_send, "zl")
    top_block = lax.all_to_all(top_part, "x", 0, 0).sum(0)
    return top_block, cross[None], child_block[None]


def solution(mesh):
    fine = Mesh(mesh.devices.reshape(SIZES), AXES)
    child = P("sub", ("x", "zl"), COLS)
    top = P(ROWS, COLS)
    return jax.shard_map(
        on_device,
        mesh=fine,
        in_specs=(top, P(), child, child),
        out_specs=(top, child, child),
        check_vma=False,
    )
```

```python
import jax
import jax.numpy as jnp
from jax import lax
from jax.experimental import pallas as pl
from jax.experimental.pallas import tpu as pltpu
from jax.sharding import Mesh, PartitionSpec as P

AXES = ("sub", "x", "zl", "y", "core")
SIZES = (2, 4, 2, 4, 2)
ROWS = ("sub", "x", "zl")
COLS = ("y", "core")
F32 = jnp.float32
VMEM_BYTES = 60 * 2**20


def along(value, axis, step):
    return lax.ppermute(value, axis, [(i, (i + step) % 4) for i in range(4)])


def along_z(value, step):
    return lax.ppermute(value, ("sub", "zl"), [(i, (i + step) % 4) for i in range(4)])


def other(value, axis):
    return lax.ppermute(value, axis, [(0, 1), (1, 0)])


def parts(value):
    high = value.astype(jnp.bfloat16)
    return high, (value - high.astype(F32)).astype(jnp.bfloat16)


def product(a, b, da, db):
    a_high, a_low = parts(a)
    b_high, b_low = parts(b)

    def one(first, second):
        return lax.dot_general(
            first, second, (((da,), (db,)), ((), ())), preferred_element_type=F32
        )

    return one(a_high, b_high) + (one(a_high, b_low) + one(a_low, b_high))


def fetch(pairs, sems):
    copies = [pltpu.make_async_copy(s, d, sems.at[i]) for i, (s, d) in enumerate(pairs)]
    for copy in copies:
        copy.start()
    return copies


def finish(copies):
    for copy in copies:
        copy.wait()


def call(kernel, where, inputs, outs, scratch, copies, indices=(), direct=()):
    n_in = len(inputs)
    smem = pl.BlockSpec(memory_space=pltpu.SMEM)
    anywhere = pl.BlockSpec(memory_space=pl.ANY)
    vmem = pl.BlockSpec(memory_space=pltpu.VMEM)
    return pl.pallas_call(
        kernel,
        out_shape=list(outs),
        in_specs=[smem] * (1 + len(indices)) + [anywhere] * n_in,
        out_specs=[anywhere if i in direct else vmem for i in range(len(outs))],
        scratch_shapes=list(scratch) + [pltpu.SemaphoreType.DMA((copies,))],
        compiler_params=pltpu.CompilerParams(vmem_limit_bytes=VMEM_BYTES),
        cost_estimate=pl.CostEstimate(flops=1, bytes_accessed=1, transcendentals=0),
    )(where, *indices, *inputs)


def shape(*dims):
    return jax.ShapeDtypeStruct(dims, F32)


def spot(where):
    return [where[i] for i in range(5)]


def select_kernel(where, index, *refs):
    pieces, (out, *sent), (stripe, picked, sems) = refs[:8], refs[8:14], refs[14:]
    sub, x, zl, y, core = spot(where)
    size, depth = pieces[0].shape
    finish(fetch([(p, stripe.at[pl.ds(i * size, size)]) for i, p in enumerate(pieces)], sems))
    half = size // 2
    pairs = []
    for i in range(5):
        target = (2 * sub + zl + i % 4) % 4
        for h in range(2):
            place = (y - 2 * (target // 2) - h + 8) % 4 + (4 if i == 4 else 0)
            row = pl.multiple_of(place * size + (target % 2) * half, half)
            pairs.append((stripe.at[pl.ds(row, half)], sent[i].at[pl.ds(h * half, half)]))
    copies = fetch(pairs, sems)

    def some(i, carry):
        found = [stripe[pl.ds(index[i * 32 + k], 1), :] for k in range(32)]
        for k in range(32):
            picked[pl.ds(i * 32 + k, 1), :] = found[k]
        return carry

    count = picked.shape[0]
    lax.fori_loop(0, count // 32, some, 0)
    order, share = count // 2, out.shape[2]
    for child in range(2):
        left = picked[pl.ds(child * order, order), :]
        start = pl.multiple_of(child * order + (2 * y + core) * share, share)
        right = picked[pl.ds(start, share), :]
        block = product(left, right, 1, 1).reshape(order // share, share, share)
        out[pl.ds(child * (order // share), order // share)] = block
    finish(copies)


def cross_kernel(where, *refs):
    covs, factors, mine, out, sent = refs[:8], refs[8:12], refs[12:16], refs[16], refs[17:21]
    held, right, turned, sems = refs[21:]
    sub, x, zl, y, core = spot(where)
    depth = right.shape[0] // 4
    pairs = [(c, held.at[i]) for i, c in enumerate(covs)]
    pairs += [(f, right.at[pl.ds(i * depth, depth)]) for i, f in enumerate(factors)]
    pairs += [(p, turned.at[(y - x - e + 8) % 4]) for e, p in enumerate(mine)]
    finish(fetch(pairs, sems))

    def block(i):
        return held[(y - x + i // 2 + 8) % 4 + jnp.where(core == i % 2, 0, 4)]

    cross = -product(jnp.concatenate([block(i) for i in range(8)], 1), right[...], 1, 0)
    out[...] = cross
    rows = out.shape[0]
    for d in range(4):
        sent[d][:rows] = cross
        sent[d][rows:] = turned[d]


def factor_kernel(where, *refs):
    panels, inverses, out, (left, right, sems) = refs[:8], refs[8:12], refs[12], refs[13:]
    sub, x, zl, y, core = spot(where)
    pairs = [
        (p, left.at[(core + i // 4) % 2, (y - i % 4 + 4) % 4]) for i, p in enumerate(panels)
    ]
    pairs += [(v, right.at[(x - i + 4) % 4]) for i, v in enumerate(inverses)]
    finish(fetch(pairs, sems))
    both = jnp.concatenate(
        [jnp.concatenate([left[p, i] for i in range(4)], 1) for p in range(2)], 0
    )
    out[...] = product(both, right[...].reshape(both.shape[1], out.shape[1]), 1, 0)


def whole_kernel(where, mine, came, both, own):
    total = mine[...] + came[...]
    both[...] = total
    rows = own.shape[0]

    @pl.when(where[2] == 0)
    def _():
        own[...] = total[:rows]

    @pl.when(where[2] == 1)
    def _():
        own[...] = total[rows:]


def fetch_left(lefts, left, core, zl, at):
    mine = jnp.where(core == zl, 0, 1)
    return [(p, left.at[(mine + i // 4) % 2, (at - i % 4 + 4) % 4]) for i, p in enumerate(lefts)]


def gram_kernel(where, *refs):
    lefts, rights, (keep, send), (left, right, sems) = refs[:8], refs[8:12], refs[12:14], refs[14:]
    sub, x, zl, y, core = spot(where)
    pairs = fetch_left(lefts, left, core, zl, x)
    pairs += [(v, right.at[(x - i + 4) % 4]) for i, v in enumerate(rights)]
    finish(fetch(pairs, sems))
    depth = right.shape[0] * right.shape[1]
    for slot, out in ((1, send), (0, keep)):
        both = jnp.concatenate([left[slot, i] for i in range(4)], 1)
        out[...] = product(both, right[...].reshape(depth, right.shape[2]), 1, 0)


def update_kernel(where, *refs):
    keep_gram, send_gram, near, far = refs[0], refs[1], refs[2:6], refs[6:10]
    keep, send, left, right, sems = refs[10:]
    sub, x, zl, y, core = spot(where)
    mine = jnp.where(core == zl, 0, 1)
    rows = right.shape[1]
    pairs = [(keep_gram, keep), (send_gram, send)]
    for d in range(4):
        place = (x - d + 4) % 4
        pairs.append((near[d].at[pl.ds(0, rows)], right.at[place]))
        pairs.append((near[d].at[pl.ds(rows, rows)], left.at[mine, place]))
        pairs.append((far[d].at[pl.ds(rows, rows)], left.at[1 - mine, place]))
    finish(fetch(pairs, sems))
    straight = right[...].reshape(4 * rows, right.shape[2])
    for slot, out in ((1, send), (0, keep)):
        both = left[slot].reshape(4 * rows, left.shape[3])
        out[...] = out[...] - product(both, straight, 0, 0)


def turn_kernel(where, *refs):
    stack, outs, (held, sems) = refs[0], refs[1:5], refs[5:]
    sub, x, zl, y, core = spot(where)
    finish(fetch([(stack.at[(x + d) % 4], held.at[d]) for d in range(4)], sems))
    finish(fetch([(held.at[d], outs[d]) for d in range(4)], sems))


def flip_kernel(value, out):
    out[...] = value[...].T


def top_kernel(where, *refs):
    lefts, rights, out, (left, right, sems) = refs[:8], refs[8], refs[9], refs[10:]
    sub, x, zl, y, core = spot(where)
    pairs = [
        (p, left.at[(core + i // 4) % 2, (2 * sub + zl - i % 4 + 4) % 4])
        for i, p in enumerate(lefts)
    ]
    finish(fetch(pairs + [(rights, right)], sems))
    rows = out.shape[1]
    for parity in range(2):
        both = jnp.concatenate([left[parity, i] for i in range(4)], 1)
        total = product(both, right[...].reshape(both.shape[1], out.shape[2]), 1, 0)
        for h in range(2):
            out[2 * h + parity] = total[h * rows : (h + 1) * rows]


def after(value, *first):
    return lax.optimization_barrier((value, *first))[0]


def on_device(top_inverse, ancestors, child_panel, child_inverse):
    sub, x, zl, y, core = (lax.axis_index(a) for a in AXES)
    where = jnp.stack([sub, x, zl, y, core]).astype(jnp.int32)
    panel = child_panel[0]
    inverse = child_inverse[0]
    rows, width = panel.shape
    stripe, block = top_inverse.shape
    order = ancestors.shape[1]
    share = order // 8

    def vmem(*dims):
        return pltpu.VMEM(dims, F32)

    def flipped(value):
        return pl.pallas_call(
            flip_kernel,
            out_shape=shape(value.shape[1], value.shape[0]),
            cost_estimate=pl.CostEstimate(flops=1, bytes_accessed=1, transcendentals=0),
        )(value)

    def over_y(value):
        return [value] + [along(value, "y", e) for e in (1, 2, 3)]

    def both_cores(values):
        return values + [other(v, "core") for v in values]

    stripes = over_y(flipped(top_inverse))
    flip = [(2 * a + c, 2 * (1 - a) + (1 - c)) for a in (0, 1) for c in (0, 1) if a != c]
    panel = jnp.where(core == zl, panel, lax.ppermute(panel, ("zl", "core"), flip))
    inverse_x = [inverse] + [along(inverse, "x", d) for d in (1, 2, 3)]
    inverse_t = flipped(inverse)
    top_z = lax.all_gather(top_inverse, ("sub", "zl"), axis=0)
    owner = ancestors // block
    place = (y - owner // 2) % 4 + jnp.where(owner % 2 == core, 0, 4)
    index = (place * block + ancestors % block).reshape(-1)
    stripes, panel, inverse_x, inverse_t, index, where = lax.optimization_barrier(
        (stripes, panel, inverse_x, inverse_t, index, where)
    )

    inverse_y = lax.all_gather(inverse_t, "y", axis=0)
    panels = over_y(panel)
    part, own0, own1, own2, own3, there0 = call(
        select_kernel, where, both_cores(stripes),
        [shape(16, share, share)] + [shape(block, stripe)] * 5,
        [vmem(8 * block, stripe), vmem(2 * order, stripe)], 10, (index,), (1, 2, 3, 4, 5),
    )
    part, own1, own2, own3, panels, top_z = lax.optimization_barrier(
        (part, own1, own2, own3, panels, top_z)
    )

    cov = lax.all_to_all(part, ROWS, 0, 0).sum(0)
    (factor_part,) = call(
        factor_kernel, where, both_cores(panels) + inverse_x,
        [shape(2 * rows, width)], [vmem(2, 4, rows, width), vmem(4, width, width)], 12,
    )
    turned = call(
        turn_kernel, where, [after(inverse_y, factor_part)], [shape(width, width)] * 4,
        [vmem(4, width, width)], 4, (), (0, 1, 2, 3),
    )
    inverse_columns = [turned[0]] + [along(turned[d], "x", d) for d in (1, 2, 3)]
    factor, factor_own = pl.pallas_call(
        whole_kernel,
        out_shape=[shape(2 * rows, width), shape(rows, width)],
        in_specs=[pl.BlockSpec(memory_space=pltpu.SMEM)]
        + [pl.BlockSpec(memory_space=pltpu.VMEM)] * 2,
        out_specs=[pl.BlockSpec(memory_space=pltpu.VMEM)] * 2,
        compiler_params=pltpu.CompilerParams(vmem_limit_bytes=VMEM_BYTES),
        cost_estimate=pl.CostEstimate(flops=1, bytes_accessed=1, transcendentals=0),
    )(where, factor_part, other(factor_part, "zl"))
    cov_y = over_y(cov)
    cov_y, factor, factor_own, own1, own2, own3, inverse_columns[0] = lax.optimization_barrier(
        (cov_y, factor, factor_own, own1, own2, own3, inverse_columns[0])
    )

    factor_x = [factor] + [along(factor, "x", d) for d in (1, 2, 3)]
    own = [own0] + [along_z(v, d + 1) for d, v in enumerate((own1, own2, own3))]
    factor_y = over_y(factor_own)
    grams = call(
        gram_kernel, where, both_cores(inverse_columns) + inverse_x, [shape(width, width)] * 2,
        [vmem(2, 4, width, width), vmem(4, width, width)], 12,
    )
    cov_y[0] = after(cov_y[0], grams[0])
    cross, *sent = call(
        cross_kernel, where, both_cores(cov_y) + factor_x + factor_y,
        [shape(rows, width)] + [shape(2 * rows, width)] * 4,
        [vmem(8, rows, share), vmem(8 * rows, width), vmem(4, rows, width)], 16,
    )
    cross, sent, grams, own = lax.optimization_barrier((cross, sent, grams, own))

    near = [sent[0]] + [along(sent[d], "x", d) for d in (1, 2, 3)]
    there = [there0] + [other(v, "core") for v in own[1:]]
    (top_part,) = call(
        top_kernel, where, own + there + [top_z], [shape(4, stripe, block)],
        [vmem(2, 4, block, stripe), vmem(4, stripe, block)], 9,
    )
    near, top_part = lax.optimization_barrier((near, top_part))

    far = [other(v, "core") for v in near]
    block_keep, block_send = call(
        update_kernel, where, list(grams) + near + far, [shape(width, width)] * 2,
        [vmem(2, 4, rows, width), vmem(4, rows, width)], 14,
    )
    child_block = block_keep + other(block_send, "zl")
    top_block = lax.all_to_all(top_part, "x", 0, 0).sum(0)
    return top_block, cross[None], child_block[None]


def solution(mesh):
    fine = Mesh(mesh.devices.reshape(SIZES), AXES)
    child = P("sub", ("x", "zl"), COLS)
    top = P(ROWS, COLS)
    return jax.shard_map(
        on_device,
        mesh=fine,
        in_specs=(top, P(), child, child),
        out_specs=(top, child, child),
        check_vma=False,
    )
```
